256 devices in a mesh: dp: 16 (over z_lo, y, core), tensor: 16 (over z_hi, x).
Axes of the slice: x: 4, y: 4, z: 8 (z_hi: 4, z_lo: 2; z = z_hi * 2 + z_lo), core: 2. Of those that a mesh axis runs over, the one named last changes fastest.
Arguments:
- query: bfloat16 [16384, 8192], P('dp', 'tensor'), may hold values from -144 to 144
- key_value: bfloat16 [2, 16384, 1024], P(None, 'dp'), may hold values from -6 to 6
- residual: bfloat16 [16384, 4096], P('dp', 'tensor'), may hold values from -2.7 to 2.7
- out_weight: bfloat16 [8192, 4096], P('tensor'), may hold values from -0.09375 to 0.09375
- norm_gain: bfloat16 [4096], replicated, may hold values from 0.099609375 to 1.8984375
- doc_ids: int32 [16, 1024], replicated, may hold values from 0 to 15, as said below
Outputs:
- hidden: bfloat16 [16384, 4096], P('dp', 'tensor')
- normed: bfloat16 [16384, 4096], P('dp', 'tensor')
The draws below stay inside these ranges and needn't reach their ends.
Inputs may be any that keep to these rules, and one draw needn't show every extreme that they name: `doc_ids`: numbers start at 0 in each row and never fall along it; every sequence has a length that is a multiple of 64; in every draw some row holds a single sequence of 1024 tokens and some row holds only sequences of 64 tokens.
All inputs are finite; a program needn't handle non-finite values.
Results may differ from the reference program's by a relative error of at most 0.017.
Values may be sent and summed in bfloat16 or wider, within the bound.
No kernel may reach another device: no remote copies, remote signals or barrier semaphores. Data moves between devices by JAX's collectives and lax.ppermute only.
A program may use at most 64 MiB of HBM per device.

```python
import math
import jax
import jax.numpy as jnp
from jax import lax

D = 4096
HEADS = 64
KVH = 8
HD = 128
MINLEN = 64
TOK_DEV = 1024
TOKENS = 16384
N_DP = 16
N_TENSOR = 16


def packing(key):
    unit_count = TOK_DEV // MINLEN
    heavy_group = jax.random.randint(jax.random.fold_in(key, 11), (), 0, N_DP)
    light_group = jnp.bitwise_xor(heavy_group, 1)
    levels = jax.random.randint(jax.random.fold_in(key, 12), (N_DP, 1), 1, 8)
    dice_rolls = jax.random.randint(jax.random.fold_in(key, 13), (N_DP, unit_count), 0, 16)
    group_ids = jnp.arange(N_DP, dtype=jnp.int32)[:, None]
    unit_ids = jnp.arange(unit_count, dtype=jnp.int32)[None, :]
    new_doc = (dice_rolls < levels).astype(jnp.int32)
    new_doc = jnp.where(group_ids == heavy_group, 0, new_doc)
    new_doc = jnp.where(group_ids == light_group, 1, new_doc)
    new_doc = jnp.where(unit_ids == 0, 0, new_doc)
    unit_docs = jnp.cumsum(new_doc, axis=1)
    return jnp.repeat(unit_docs, MINLEN, axis=1).astype(jnp.int32)


def key_base(key):
    return jnp.clip(jax.random.normal(key, (TOKENS, KVH * HD), jnp.float32), -6.0, 6.0)


def draw_doc_ids(key, part):
    packed = packing(key)
    return packed


def draw_query(key, part):
    key = jax.random.fold_in(key, 5)
    base_draw = 2.0 * jnp.clip(jax.random.normal(key, (TOKENS, HEADS * HD), jnp.float32), -6.0, 6.0)
    return base_draw.astype(jnp.bfloat16)


def draw_key_value(key, part):
    base_keys = key_base(key)
    key = jax.random.fold_in(key, 3)
    values = jnp.clip(jax.random.normal(key, (TOKENS, KVH * HD), jnp.float32), -6.0, 6.0)
    return jnp.stack([base_keys, values]).astype(jnp.bfloat16)


def draw_residual(key, part):
    key = jax.random.fold_in(key, 7)
    column_pos = jnp.arange(D, dtype=jnp.float32) / D
    noise_draw = jnp.clip(jax.random.normal(key, (TOKENS, D), jnp.float32), -6.0, 6.0)
    column_scale = 0.15 * 3.0 ** column_pos
    return (noise_draw * column_scale[None, :]).astype(jnp.bfloat16)


def raised(values, key, source, target, parts, factor):
    def block_of(dim):
        return (jnp.arange(values.shape[dim]) // (values.shape[dim] // parts)).reshape((-1,) + (1,) * (values.ndim - 1 - dim))

    near = jax.random.permutation(key, parts)[block_of(target)]
    second = (block_of(target) + parts // 2) % parts
    return jnp.where((block_of(source) == near) | (block_of(source) == second), factor * values, values)


def block_levels(rng, dims, cuts, low, high):
    factor_of = 1.0
    for position, blocks in cuts:
        steps = jax.random.uniform(jax.random.fold_in(jax.random.fold_in(rng, 6), position), (blocks,), jnp.float32, low / len(cuts), high / len(cuts))
        factor_of = factor_of * jnp.repeat(jnp.exp(steps), dims[position] // blocks).reshape((-1,) + (1,) * (len(dims) - 1 - position))
    return factor_of


def noise_with(rng, shape, scale, reach, cuts, heavy, kind=jnp.bfloat16):
    result = scale * jax.random.normal(rng, shape, jnp.float32)
    if cuts:
        result = result * block_levels(rng, shape, cuts, -0.22, 0.18)
    return jnp.clip(raised(result, jax.random.fold_in(rng, 3), *heavy), -reach, reach).astype(kind)


def setup_inputs(seed: int = 0) -> dict:
    keys = jax.random.split(jax.random.key(seed), 7)
    query = draw_query(jax.random.fold_in(keys[6], 71), 0)
    key_value = draw_key_value(jax.random.fold_in(keys[6], 71), 0)
    residual = draw_residual(jax.random.fold_in(keys[6], 71), 0)
    out_weight = noise_with(keys[3], (HEADS * HD, D), (HEADS * HD) ** -0.5, 0.09375, ((0, 16),), (0, 1, 16, 2.0))
    norm_gain = jnp.clip(1.0 + 0.18 * jax.random.normal(keys[4], (D,), jnp.float32), 0.099609375, 1.8984375).astype(jnp.bfloat16)
    doc_ids = draw_doc_ids(jax.random.fold_in(keys[6], 71), 0)
    return {"query": query, "key_value": key_value, "residual": residual, "out_weight": out_weight, "norm_gain": norm_gain, "doc_ids": doc_ids}


MASK_FILL = -1e+30
EPSILON = 1e-06

def group_attention(group_query, group_keys, group_values, group_docs):
    positions = jnp.arange(TOK_DEV, dtype=jnp.int32)
    allowed = (group_docs[:, None] == group_docs[None, :]) & (positions[None, :] <= positions[:, None])
    per_kv = HEADS // KVH
    score_scale = 1.0 / math.sqrt(HD)

    def one_head(head_index):
        kv_column = head_index // per_kv * HD
        head_query = lax.dynamic_slice_in_dim(group_query, head_index * HD, HD, 1)
        head_keys = lax.dynamic_slice_in_dim(group_keys, kv_column, HD, 1)
        head_values = lax.dynamic_slice_in_dim(group_values, kv_column, HD, 1)
        scores = jnp.dot(head_query, head_keys.T, preferred_element_type=jnp.float32) * score_scale
        scores = jnp.where(allowed, scores, MASK_FILL)
        top_score = lax.optimization_barrier(jnp.max(scores, axis=1, keepdims=True))
        weights = jnp.where(allowed, jnp.exp(scores - top_score), 0.0)
        weight_sum = lax.optimization_barrier(jnp.sum(weights, axis=1, keepdims=True))
        summed = jnp.dot(weights.astype(jnp.bfloat16), head_values, preferred_element_type=jnp.float32)
        return (summed / weight_sum).astype(jnp.bfloat16)
    per_head = lax.map(one_head, jnp.arange(HEADS, dtype=jnp.int32))
    return per_head.transpose(1, 0, 2).reshape(TOK_DEV, HEADS * HD)

def reference(query, key_value, residual, out_weight, norm_gain, doc_ids):
    per_device = HEADS // N_TENSOR
    query_groups = query.reshape(N_DP, TOK_DEV, HEADS * HD)
    key_groups = key_value[0].reshape(N_DP, TOK_DEV, KVH * HD)
    value_groups = key_value[1].reshape(N_DP, TOK_DEV, KVH * HD)
    residual_groups = residual.reshape(N_DP, TOK_DEV, D)
    weight_pieces = out_weight.reshape(N_TENSOR, per_device * HD, D)
    gain_wide = norm_gain.astype(jnp.float32)

    def one_group(inputs):
        group_query, group_keys, group_values, group_residual, group_docs = inputs
        attention = group_attention(group_query, group_keys, group_values, group_docs)
        pieces = attention.reshape(TOK_DEV, N_TENSOR, per_device * HD).transpose(1, 0, 2)

        def add_piece(summed, piece_pair):
            piece_rows, piece_weight = piece_pair
            term = jnp.dot(piece_rows, piece_weight, preferred_element_type=jnp.float32).astype(jnp.bfloat16)
            term = lax.optimization_barrier(term)
            return (summed + term.astype(jnp.float32), None)
        mixed, _ = lax.scan(add_piece, jnp.zeros((TOK_DEV, D), jnp.float32), (pieces, weight_pieces))
        hidden = (group_residual.astype(jnp.float32) + mixed).astype(jnp.bfloat16)
        widened = hidden.astype(jnp.float32)
        inverse_rms = lax.rsqrt(lax.optimization_barrier(jnp.mean(widened * widened, axis=1, keepdims=True)) + EPSILON)
        normed = (widened * inverse_rms * gain_wide).astype(jnp.bfloat16)
        return (hidden, normed)
    hidden, normed = lax.map(one_group, (query_groups, key_groups, value_groups, residual_groups, doc_ids))
    return (hidden.reshape(TOKENS, D), normed.reshape(TOKENS, D))
```

```python
import functools, math

import jax
import jax.numpy as jnp
from jax import lax
from jax.experimental import pallas as pl
from jax.experimental.pallas import tpu as pltpu
from jax.sharding import PartitionSpec as P

D = 4096
HEADS = 64
KVH = 8
HD = 128
SUB = 256
X = 4
Z = 4
MASK_FILL = -1e30
EPSILON = 1e-06
PLAN = {"B": (0, 448, "x", 1, True), "A": (448, 256, "z", 1, True), "C": (704, 320, "x", -1, False)}
ORDER = ("1B", "1A", "1C", "2B", "2A", "2C", "3B", "3A", "3C", "FB", "FC", "FA")
GATES = {("C", 1, "back"): "3B", ("A", 2, 0): "FB"}
COST = pl.CostEstimate(flops=1, bytes_accessed=1, transcendentals=0)
LONG = pl.CostEstimate(flops=200_000_000_000, bytes_accessed=1, transcendentals=0)
PROJECT_VMEM = 36 << 20
OTHER_VMEM = 16 << 20


def ring_pairs(axis, step):
    pairs = []
    for z in range(Z):
        for x in range(X):
            to = z * X + (x + step) % X if axis == "x" else (z + step) % Z * X + x
            pairs.append((z * X + x, to))
    return pairs


def shift(value, axis, step):
    return lax.ppermute(value, "tensor", ring_pairs(axis, step))


def place_of(axis, where):
    return where[3] if axis == "x" else where[2]


def attend_rows(first, rows, docs, q_ref, q_first, kv_ref):
    factor = math.log2(math.e) / math.sqrt(HD)
    q_docs = jnp.broadcast_to(docs[:, first : first + rows], (128, rows)).T[:, :1]
    tiles = [(start, min(SUB, first - start)) for start in range(0, first, SUB)] + [(first, rows)]
    masks = []
    for start, width in tiles:
        mask = q_docs == docs[:, start : start + width]
        if start == first:
            here = (rows, width)
            mask = mask & (lax.broadcasted_iota(jnp.int32, here, 1) <= lax.broadcasted_iota(jnp.int32, here, 0))
        masks.append(mask)
    heads = []
    for head in range(q_ref.shape[1] // HD):
        q = q_ref[q_first : q_first + rows, head * HD : (head + 1) * HD]
        scores = []
        peak = None
        for (start, width), mask in zip(tiles, masks):
            keys = kv_ref[0, start : start + width, :]
            score = lax.dot_general(q, keys, (((1,), (1,)), ((), ())), preferred_element_type=jnp.float32)
            score = jnp.where(mask, score, MASK_FILL)
            top = jnp.max(score, axis=1, keepdims=True)
            peak = top if peak is None else jnp.maximum(peak, top)
            scores.append(score)
        offset = peak * factor
        total = 0.0
        summed = 0.0
        for (start, width), score in zip(tiles, scores):
            weight = jnp.exp2(score * factor - offset)
            total = total + jnp.sum(weight, axis=1, keepdims=True)
            summed = summed + jnp.dot(
                weight.astype(jnp.bfloat16), kv_ref[1, start : start + width, :], preferred_element_type=jnp.float32
            )
        heads.append((summed / total).astype(jnp.bfloat16))
    return jnp.concatenate(heads, axis=1)


def project_kernel(first, rows, axis, where_ref, docs_hbm, q_hbm, kv_hbm, w_hbm, token_ref, *rest):
    outs, (token_out, docs_ref, q_ref, kv_ref, w_ref, attn_ref, sems) = rest[:-7], rest[-7:]
    keys = kv_ref.shape[1]
    column = pl.ds(pl.multiple_of(where_ref[0] * HD, HD), HD)
    fetches = [
        pltpu.make_async_copy(docs_hbm, docs_ref, sems.at[0]),
        pltpu.make_async_copy(q_hbm.at[pl.ds(first, rows), :], q_ref, sems.at[1]),
        pltpu.make_async_copy(kv_hbm.at[:, pl.ds(0, keys), column], kv_ref, sems.at[2]),
        pltpu.make_async_copy(w_hbm, w_ref, sems.at[3]),
    ]
    for fetch in fetches:
        fetch.start()
    token_out[...] = jnp.zeros_like(token_out)
    for fetch in fetches[:3]:
        fetch.wait()
    docs = docs_ref[pl.ds(where_ref[1], 1), :]
    for at in range(0, rows, SUB):
        size = min(SUB, rows - at)
        attn_ref[at : at + size, :] = attend_rows(first + at, size, docs, q_ref, at, kv_ref)
    fetches[3].wait()
    attn = attn_ref[...]
    wide = w_ref.shape[1] // (X * Z)
    for step in (2, 3, 1, 0):
        if axis == "x":
            place = lax.rem(where_ref[3] + step, X)
            for z in range(Z):
                cols = pl.ds(pl.multiple_of((z * X + place) * wide, wide), wide)
                outs[step][:, z * wide : (z + 1) * wide] = jnp.dot(
                    attn, w_ref[:, cols], preferred_element_type=jnp.float32
                ).astype(jnp.bfloat16)
        else:
            place = lax.rem(where_ref[2] + step, Z)
            cols = pl.ds(pl.multiple_of(place * (X * wide), X * wide), X * wide)
            outs[step][...] = jnp.dot(attn, w_ref[:, cols], preferred_element_type=jnp.float32).astype(jnp.bfloat16)


TOKEN = jax.ShapeDtypeStruct((8, 128), jnp.float32)
TOKEN_SPEC = pl.BlockSpec((8, 128), lambda i, s: (0, 0))


def project(first, rows, axis, where, docs, query, key_value, out_weight, token):
    cols = query.shape[1]
    keys = first + rows
    docs, query, key_value, out_weight = [
        pltpu.with_memory_space_constraint(a, pltpu.HBM) for a in (docs, query, key_value, out_weight)
    ]
    count = 4
    wide = out_weight.shape[1] // count
    *blocks, token = pl.pallas_call(
        functools.partial(project_kernel, first, rows, axis),
        out_shape=[jax.ShapeDtypeStruct((rows, wide), jnp.bfloat16)] * count + [TOKEN],
        grid_spec=pltpu.PrefetchScalarGridSpec(
            num_scalar_prefetch=1,
            grid=(1,),
            in_specs=[pl.BlockSpec(memory_space=pltpu.HBM)] * 4 + [pl.BlockSpec(memory_space=pl.ANY)],
            out_specs=[pl.BlockSpec((rows, wide), lambda i, s: (0, 0))] * count + [TOKEN_SPEC],
            scratch_shapes=[
                pltpu.VMEM(docs.shape, jnp.int32),
                pltpu.VMEM((rows, cols), jnp.bfloat16),
                pltpu.VMEM((2, keys, HD), jnp.bfloat16),
                pltpu.VMEM(out_weight.shape, jnp.bfloat16),
                pltpu.VMEM((rows, cols), jnp.bfloat16),
                pltpu.SemaphoreType.DMA((4,)),
            ],
        ),
        compiler_params=pltpu.CompilerParams(vmem_limit_bytes=PROJECT_VMEM),
        cost_estimate=COST,
        name="project_%d" % first,
    )(where, docs, query, key_value, out_weight, token)
    return blocks, token


def add_kernel(token_ref, a_ref, b_ref, out_ref, token_out):
    token_out[...] = jnp.zeros_like(token_out)
    out_ref[...] = (a_ref[...].astype(jnp.float32) + b_ref[...].astype(jnp.float32)).astype(jnp.bfloat16)


def add(a, b, cost, token):
    whole = pl.BlockSpec(a.shape, lambda i: (0, 0))
    return pl.pallas_call(
        add_kernel,
        out_shape=[jax.ShapeDtypeStruct(a.shape, jnp.bfloat16), TOKEN],
        grid=(1,),
        in_specs=[pl.BlockSpec(memory_space=pl.ANY), whole, whole],
        out_specs=[whole, pl.BlockSpec((8, 128), lambda i: (0, 0))],
        compiler_params=pltpu.CompilerParams(vmem_limit_bytes=OTHER_VMEM),
        cost_estimate=cost,
        name="add",
    )(token, a, b)


def merge_kernel(axis, wide, together, where_ref, token_ref, *refs):
    ins, outs = refs[:3], refs[3:]
    outs[-1][...] = jnp.zeros_like(outs[-1])
    for step in range(4):
        if together:
            cols = pl.ds(step * wide, wide)
        elif axis == "x":
            cols = pl.ds(pl.multiple_of(lax.rem(where_ref[3] + step, X) * wide, wide), wide)
        else:
            cols = pl.ds(pl.multiple_of(lax.rem(where_ref[2] + step, Z) * wide, wide), wide)
        total = ins[0][:, cols].astype(jnp.float32)
        for ref in ins[1:]:
            total = total + ref[:, cols].astype(jnp.float32)
        if together:
            outs[0][step] = total.astype(jnp.bfloat16)
        else:
            outs[step][...] = total.astype(jnp.bfloat16)


def merge(axis, where, total, others, together, cost, token):
    rows, cols = total.shape
    wide = cols // 4
    whole = pl.BlockSpec((rows, cols), lambda i, s: (0, 0))
    shapes = [(4, rows, wide)] if together else [(rows, wide)] * 4
    *blocks, token = pl.pallas_call(
        functools.partial(merge_kernel, axis, wide, together),
        out_shape=[jax.ShapeDtypeStruct(shape, jnp.bfloat16) for shape in shapes] + [TOKEN],
        grid_spec=pltpu.PrefetchScalarGridSpec(
            num_scalar_prefetch=1,
            grid=(1,),
            in_specs=[pl.BlockSpec(memory_space=pl.ANY)] + [whole] * (1 + len(others)),
            out_specs=[pl.BlockSpec(shape, lambda i, s, n=len(shape): (0,) * n) for shape in shapes] + [TOKEN_SPEC],
        ),
        compiler_params=pltpu.CompilerParams(vmem_limit_bytes=OTHER_VMEM),
        cost_estimate=cost,
        name="merge",
    )(where, token, total, *others)
    return blocks, token


def final_kernel(token_ref, residual_ref, *rest):
    others, (hidden_ref, squares_ref, token_out) = rest[:-3], rest[-3:]
    token_out[...] = jnp.zeros_like(token_out)
    parts = [others[0][i] for i in range(4)] if len(others) == 1 else [ref[...] for ref in others]
    mixed = parts[0].astype(jnp.float32)
    for part in parts[1:]:
        mixed = mixed + part.astype(jnp.float32)
    hidden = (residual_ref[...].astype(jnp.float32) + mixed).astype(jnp.bfloat16)
    hidden_ref[...] = hidden
    widened = hidden.astype(jnp.float32)
    squares_ref[...] = jnp.sum(widened * widened, axis=1, keepdims=True)


def final(first, residual, blocks, token):
    rows, cols = blocks[0].shape[-2:]
    whole = pl.BlockSpec((rows, cols), lambda i: (0, 0))
    return pl.pallas_call(
        final_kernel,
        out_shape=[
            jax.ShapeDtypeStruct((rows, cols), jnp.bfloat16),
            jax.ShapeDtypeStruct((rows, 1), jnp.float32),
            TOKEN,
        ],
        grid=(1,),
        in_specs=[pl.BlockSpec(memory_space=pl.ANY)]
        + [pl.BlockSpec((pl.Element(rows), pl.Element(cols)), lambda i: (first, 0))]
        + [pl.BlockSpec(b.shape, lambda i, n=b.ndim: (0,) * n) for b in blocks],
        out_specs=[whole, pl.BlockSpec((rows, 1), lambda i: (0, 0)), pl.BlockSpec((8, 128), lambda i: (0, 0))],
        compiler_params=pltpu.CompilerParams(vmem_limit_bytes=OTHER_VMEM),
        cost_estimate=COST,
        name="final",
    )(token, residual, *blocks)


def swap(value, axis):
    if axis == "x":
        groups = [[z * X + x for x in range(X)] for z in range(Z)]
    else:
        groups = [[z * X + x for z in range(Z)] for x in range(X)]
    return lax.all_to_all(value, "tensor", split_axis=0, concat_axis=0, axis_index_groups=groups, tiled=True)


class Sender:
    def __init__(self):
        self.tokens = {}
        self.held = {}
        self.results = {}

    def send(self, name, value, axis, way):
        gate = GATES.get(name)
        if gate is None or gate in self.tokens:
            if gate is not None:
                value, _ = lax.optimization_barrier((value, self.tokens[gate]))
            self.results[name] = shift(value, axis, way) if way else swap(value, axis)
        else:
            self.held[name] = (value, axis, way)

    def passed(self, step, token):
        self.tokens[step] = token
        for name in list(self.held):
            if GATES[name] == step:
                self.send(name, *self.held.pop(name))

    def take(self, *names):
        return [self.results[name] for name in names]


def body(query, key_value, residual, out_weight, norm_gain, doc_ids):
    tensor_index = lax.axis_index("tensor")
    group_index = lax.axis_index("dp")
    heads_here = query.shape[1] // HD
    kv_head = tensor_index * heads_here // (HEADS // KVH)
    where = jnp.stack([kv_head, group_index, tensor_index // X, tensor_index % X]).astype(jnp.int32)
    feature_count = residual.shape[1]
    token = where
    state = {}
    sender = Sender()
    for step, chunk in ORDER:
        first, rows, axis, way, together = PLAN[chunk]
        other = "z" if axis == "x" else "x"
        if step == "1":
            blocks, token = project(first, rows, axis, where, doc_ids, query, key_value, out_weight, token)
            near, far, back = (blocks[1], blocks[2], blocks[3]) if way > 0 else (blocks[3], blocks[2], blocks[1])
            sender.send((chunk, 1, "far"), far, axis, way)
            sender.send((chunk, 1, "back"), back, axis, -way)
            state[chunk] = (near, blocks[0])
        elif step == "2":
            near, own = state[chunk]
            if chunk == "B":
                near, _ = lax.optimization_barrier((near, *sender.take((chunk, 1, "back"))))
            summed, token = add(near, *sender.take((chunk, 1, "far")), LONG if chunk == "A" else COST, token)
            state[chunk] = own
            sender.send((chunk, 1, "near"), summed, axis, way)
        elif step == "3":
            others = sender.take((chunk, 1, "near"), (chunk, 1, "back"))
            blocks, token = merge(other, where, state[chunk], others, together, LONG if chunk == "A" else COST, token)
            if together:
                sender.send((chunk, 2, 0), blocks[0], other, 0)
            else:
                for i in (1, 3, 2):
                    sender.send((chunk, 2, i), blocks[i], other, i)
            state[chunk] = blocks[0]
        else:
            if together:
                blocks = sender.take((chunk, 2, 0))
            else:
                blocks = [state[chunk], *sender.take((chunk, 2, 1), (chunk, 2, 3), (chunk, 2, 2))]
            hidden, squares, token = final(first, residual, blocks, token)
            state[chunk] = (first, hidden, squares)
        sender.passed(step + chunk, token)
    done = sorted(state.values(), key=lambda entry: entry[0])
    hidden = jnp.concatenate([h for _, h, _ in done], axis=0)
    squares = jnp.concatenate([s for _, _, s in done], axis=0)[:, 0]
    widened = hidden.astype(jnp.float32)
    spread = jnp.broadcast_to(squares[None], (X * Z, squares.shape[0]))
    squares = jnp.sum(lax.all_to_all(spread, "tensor", split_axis=0, concat_axis=0, tiled=True), axis=0)
    gain_part = lax.dynamic_slice_in_dim(norm_gain, tensor_index * feature_count, feature_count, 0)
    normed = (
        widened * lax.rsqrt(squares / D + EPSILON)[:, None] * gain_part.astype(jnp.float32)
    ).astype(jnp.bfloat16)
    return (hidden, normed)


def solution(mesh):
    placed = (P("dp", "tensor"), P(None, "dp", None), P("dp", "tensor"), P("tensor", None), P(), P())
    return jax.shard_map(
        body, mesh=mesh, in_specs=placed, out_specs=(P("dp", "tensor"), P("dp", "tensor")), check_vma=False
    )
```

```python
import functools
import math

import jax
import jax.numpy as jnp
from jax import lax
from jax.experimental import pallas as pl
from jax.experimental.pallas import tpu as pltpu
from jax.sharding import PartitionSpec as P

D = 4096
HEADS = 64
KVH = 8
HD = 128
SUB = 256
X = 4
Z = 4
WIDE = 256
MASK_FILL = -1e30
EPSILON = 1e-06
PLAN = {"B": (0, 400, "x", 1, True), "A": (400, 224, "z", 1, False), "C": (624, 400, "x", -1, False)}
ORDER = ("1B", "1A", "1C", "2B", "2A", "2C", "3B", "3A", "3C", "FB", "FA", "FC")
GATES = {("C", 1, "back"): "2C", ("A", 2, 1): "3C", ("A", 2, 2): "3C", ("A", 2, 3): "3C"}
COST = pl.CostEstimate(flops=1, bytes_accessed=1, transcendentals=0)
LONG = pl.CostEstimate(flops=200_000_000_000, bytes_accessed=1, transcendentals=0)
ATTEND_VMEM = 36 << 20
OTHER_VMEM = 16 << 20
TOKEN = jax.ShapeDtypeStruct((8, 128), jnp.float32)
ANY = pl.BlockSpec(memory_space=pl.ANY)
OWN, NEAR, FAR, BACK = 0, 1, 2, 3


def ring_pairs(axis, step):
    pairs = []
    for z in range(Z):
        for x in range(X):
            to = z * X + (x + step) % X if axis == "x" else (z + step) % Z * X + x
            pairs.append((z * X + x, to))
    return pairs


def shift(value, axis, step):
    return lax.ppermute(value, "tensor", ring_pairs(axis, step))


def swap(value, axis):
    if axis == "x":
        groups = [[z * X + x for x in range(X)] for z in range(Z)]
    else:
        groups = [[z * X + x for z in range(Z)] for x in range(X)]
    return lax.all_to_all(value, "tensor", split_axis=0, concat_axis=0, axis_index_groups=groups, tiled=True)


def full(shape):
    return pl.BlockSpec(shape, lambda i, s: (0,) * len(shape))


def call(kernel, name, cost, vmem, where, inputs, in_specs, out_shapes, scratch=()):
    return pl.pallas_call(
        kernel,
        out_shape=out_shapes,
        grid_spec=pltpu.PrefetchScalarGridSpec(
            num_scalar_prefetch=1,
            grid=(1,),
            in_specs=in_specs,
            out_specs=[full(o.shape) for o in out_shapes],
            scratch_shapes=list(scratch),
        ),
        compiler_params=pltpu.CompilerParams(vmem_limit_bytes=vmem),
        cost_estimate=cost,
        name=name,
    )(where, *inputs)


def columns_of(where_ref, axis, way, block):
    size = X if axis == "x" else Z
    steps = block if way > 0 else (size - block) % size
    place = lax.rem(where_ref[3 if axis == "x" else 2] + steps, size)
    if axis == "x":
        return [(pl.multiple_of((z * X + place) * WIDE, WIDE), WIDE, z * WIDE) for z in range(Z)]
    return [(pl.multiple_of(place * (X * WIDE), X * WIDE), X * WIDE, 0)]


def attend_rows(first, rows, docs, q_ref, q_first, kv_ref):
    factor = math.log2(math.e) / math.sqrt(HD)
    q_docs = jnp.broadcast_to(docs[:, first : first + rows], (128, rows)).T[:, :1]
    tiles = [(start, min(SUB, first + rows - start)) for start in range(0, first + rows, SUB)]
    masks = []
    for start, width in tiles:
        mask = q_docs == docs[:, start : start + width]
        if start + width > first:
            here = (rows, width)
            ahead = lax.broadcasted_iota(jnp.int32, here, 1) - lax.broadcasted_iota(jnp.int32, here, 0)
            mask = mask & (ahead <= first - start)
        masks.append(mask)
    heads = []
    for head in range(q_ref.shape[1] // HD):
        q = q_ref[q_first : q_first + rows, head * HD : (head + 1) * HD]
        scores = []
        peak = None
        for (start, width), mask in zip(tiles, masks):
            keys = kv_ref[0, start : start + width, :]
            score = lax.dot_general(q, keys, (((1,), (1,)), ((), ())), preferred_element_type=jnp.float32)
            score = jnp.where(mask, score, MASK_FILL)
            top = jnp.max(score, axis=1, keepdims=True)
            peak = top if peak is None else jnp.maximum(peak, top)
            scores.append(score)
        offset = peak * factor
        total = 0.0
        summed = 0.0
        for (start, width), score in zip(tiles, scores):
            weight = jnp.exp2(score * factor - offset)
            total = total + jnp.sum(weight, axis=1, keepdims=True)
            summed = summed + jnp.dot(
                weight.astype(jnp.bfloat16), kv_ref[1, start : start + width, :], preferred_element_type=jnp.float32
            )
        heads.append((summed / total).astype(jnp.bfloat16))
    return jnp.concatenate(heads, axis=1)


def attend_kernel(first, rows, axis, way, inside, where_ref, token_ref, docs_hbm, q_hbm, kv_hbm, w_any, *rest):
    attn_ref, far_ref, back_ref, token_out, docs_ref, q_ref, kv_ref, sems, *more = rest
    keys = kv_ref.shape[1]
    column = pl.ds(pl.multiple_of(where_ref[0] * HD, HD), HD)
    fetches = [
        pltpu.make_async_copy(docs_hbm, docs_ref, sems.at[0]),
        pltpu.make_async_copy(q_hbm.at[pl.ds(first, rows), :], q_ref, sems.at[1]),
        pltpu.make_async_copy(kv_hbm.at[:, pl.ds(0, keys), column], kv_ref, sems.at[2]),
    ]
    for fetch in fetches:
        fetch.start()
    pieces = [columns_of(where_ref, axis, way, block) for block in (FAR, BACK)]
    later = [[], []]
    if not inside:
        w_ref, w_sems = more
        for slot in range(2):
            for i, (start, size, offset) in enumerate(pieces[slot]):
                later[slot].append(
                    pltpu.make_async_copy(
                        w_any.at[:, pl.ds(start, size)], w_ref.at[slot, :, offset : offset + size], w_sems.at[slot, i]
                    )
                )
                later[slot][-1].start()
    token_out[...] = jnp.zeros_like(token_out)
    for fetch in fetches:
        fetch.wait()
    docs = docs_ref[pl.ds(where_ref[1], 1), :]
    for at in range(0, rows, SUB):
        size = min(SUB, rows - at)
        attn_ref[at : at + size, :] = attend_rows(first + at, size, docs, q_ref, at, kv_ref)
    attn = attn_ref[...]
    for slot, out_ref in enumerate((far_ref, back_ref)):
        for fetch in later[slot]:
            fetch.wait()
        for start, size, offset in pieces[slot]:
            weight = w_any[:, pl.ds(start, size)] if inside else w_ref[slot, :, offset : offset + size]
            out_ref[:, offset : offset + size] = jnp.dot(attn, weight, preferred_element_type=jnp.float32).astype(
                jnp.bfloat16
            )


def attend(first, rows, axis, way, inside, where, docs, query, key_value, out_weight, token):
    cols = query.shape[1]
    keys = first + rows
    wide = out_weight.shape[1] // 4
    docs, query, key_value = [pltpu.with_memory_space_constraint(a, pltpu.HBM) for a in (docs, query, key_value)]
    out_weight = pltpu.with_memory_space_constraint(out_weight, pltpu.VMEM if inside else pltpu.HBM)
    scratch = [
        pltpu.VMEM(docs.shape, jnp.int32),
        pltpu.VMEM((rows, cols), jnp.bfloat16),
        pltpu.VMEM((2, keys, HD), jnp.bfloat16),
        pltpu.SemaphoreType.DMA((3,)),
    ]
    if not inside:
        scratch += [pltpu.VMEM((2, cols, wide), jnp.bfloat16), pltpu.SemaphoreType.DMA((2, 4))]
    return call(
        functools.partial(attend_kernel, first, rows, axis, way, inside),
        "attend_%d" % first,
        COST,
        ATTEND_VMEM,
        where,
        (token, docs, query, key_value, out_weight),
        [ANY] * 4 + [pl.BlockSpec(memory_space=pltpu.VMEM) if inside else ANY],
        [jax.ShapeDtypeStruct((rows, cols), jnp.bfloat16)]
        + [jax.ShapeDtypeStruct((rows, wide), jnp.bfloat16)] * 2
        + [TOKEN],
        scratch,
    )


def near_kernel(axis, way, where_ref, token_ref, w_ref, attn_ref, passed_ref, out_ref, own_ref, token_out):
    token_out[...] = jnp.zeros_like(token_out)
    for block in (NEAR, OWN):
        for start, size, offset in columns_of(where_ref, axis, way, block):
            total = jnp.dot(attn_ref[...], w_ref[:, pl.ds(start, size)], preferred_element_type=jnp.float32)
            if block == NEAR:
                total = total + passed_ref[:, offset : offset + size].astype(jnp.float32)
                out_ref[:, offset : offset + size] = total.astype(jnp.bfloat16)
            else:
                own_ref[:, offset : offset + size] = total.astype(jnp.bfloat16)


def near(axis, way, cost, where, out_weight, attn, passed, token):
    return call(
        functools.partial(near_kernel, axis, way),
        "near",
        cost,
        OTHER_VMEM,
        where,
        (token, pltpu.with_memory_space_constraint(out_weight, pltpu.VMEM), attn, passed),
        [ANY, pl.BlockSpec(memory_space=pltpu.VMEM), full(attn.shape), full(passed.shape)],
        [jax.ShapeDtypeStruct(passed.shape, jnp.bfloat16)] * 2 + [TOKEN],
    )


def merge_kernel(axis, together, where_ref, token_ref, own_ref, ahead_ref, behind_ref, *outs):
    outs[-1][...] = jnp.zeros_like(outs[-1])
    for step in range(4):
        place = step if together else lax.rem(where_ref[2 if axis == "x" else 3] + step, 4)
        cols = pl.ds(pl.multiple_of(place * WIDE, WIDE), WIDE)
        total = own_ref[:, cols].astype(jnp.float32)
        for ref in (ahead_ref, behind_ref):
            total = total + ref[:, cols].astype(jnp.float32)
        if together:
            outs[0][step] = total.astype(jnp.bfloat16)
        else:
            outs[step][...] = total.astype(jnp.bfloat16)


def merge(axis, together, cost, where, own, ahead, behind, token):
    rows = own.shape[0]
    if together:
        blocks = [jax.ShapeDtypeStruct((4, rows, WIDE), jnp.bfloat16)]
    else:
        blocks = [jax.ShapeDtypeStruct((rows, WIDE), jnp.bfloat16)] * 4
    return call(
        functools.partial(merge_kernel, axis, together),
        "merge",
        cost,
        OTHER_VMEM,
        where,
        (token, own, ahead, behind),
        [ANY] + [full(own.shape)] * 3,
        blocks + [TOKEN],
    )


def final_kernel(where_ref, token_ref, residual_ref, parts_ref, *rest):
    others, (hidden_ref, squares_ref, token_out) = rest[:-3], rest[-3:]
    token_out[...] = jnp.zeros_like(token_out)
    if others:
        mixed = parts_ref[...].astype(jnp.float32)
        for ref in others:
            mixed = mixed + ref[...].astype(jnp.float32)
    else:
        mixed = parts_ref[0].astype(jnp.float32)
        for i in range(1, 4):
            mixed = mixed + parts_ref[i].astype(jnp.float32)
    hidden = (residual_ref[...].astype(jnp.float32) + mixed).astype(jnp.bfloat16)
    hidden_ref[...] = hidden
    widened = hidden.astype(jnp.float32)
    squares_ref[...] = jnp.sum(widened * widened, axis=1, keepdims=True)


def final(first, where, residual, parts, others, token):
    rows, cols = parts.shape[-2:]
    return call(
        final_kernel,
        "final",
        COST,
        OTHER_VMEM,
        where,
        (token, pltpu.with_memory_space_constraint(residual, pltpu.HBM), parts, *others),
        [ANY, pl.BlockSpec((pl.Element(rows), pl.Element(cols)), lambda i, s: (first, 0))]
        + [full(a.shape) for a in (parts, *others)],
        [jax.ShapeDtypeStruct((rows, cols), jnp.bfloat16), jax.ShapeDtypeStruct((rows, 1), jnp.float32), TOKEN],
    )


class Sender:
    def __init__(self):
        self.tokens = {}
        self.held = {}
        self.results = {}

    def send(self, name, value, axis, way):
        gate = GATES.get(name)
        if gate is None or gate in self.tokens:
            if gate is not None:
                value, _ = lax.optimization_barrier((value, self.tokens[gate]))
            self.results[name] = shift(value, axis, way) if way else swap(value, axis)
        else:
            self.held[name] = (value, axis, way)

    def passed(self, step, token):
        self.tokens[step] = token
        for name in list(self.held):
            if GATES[name] == step:
                self.send(name, *self.held.pop(name))

    def take(self, *names):
        return [self.results[name] for name in names]


def body(query, key_value, residual, out_weight, norm_gain, doc_ids):
    tensor_index = lax.axis_index("tensor")
    group_index = lax.axis_index("dp")
    heads_here = query.shape[1] // HD
    kv_head = tensor_index * heads_here // (HEADS // KVH)
    where = jnp.stack([kv_head, group_index, tensor_index // X, tensor_index % X]).astype(jnp.int32)
    feature_count = residual.shape[1]
    token = where
    state = {}
    sender = Sender()
    for step, chunk in ORDER:
        first, rows, axis, way, together = PLAN[chunk]
        other = "z" if axis == "x" else "x"
        cost = LONG if chunk == "A" else COST
        if step == "1":
            inside = token is not where
            attn, far, back, token = attend(
                first, rows, axis, way, inside, where, doc_ids, query, key_value, out_weight, token
            )
            sender.send((chunk, 1, "far"), far, axis, way)
            sender.send((chunk, 1, "back"), back, axis, -way)
            state[chunk] = attn
        elif step == "2":
            attn = state[chunk]
            if chunk == "B":
                attn, _ = lax.optimization_barrier((attn, *sender.take((chunk, 1, "back"))))
            passed = sender.take((chunk, 1, "far"))
            summed, state[chunk], token = near(axis, way, cost, where, out_weight, attn, *passed, token)
            sender.send((chunk, 1, "near"), summed, axis, way)
        elif step == "3":
            others = sender.take((chunk, 1, "near"), (chunk, 1, "back"))
            *blocks, token = merge(axis, together, cost, where, state[chunk], *others, token)
            if together:
                sender.send((chunk, 2, 0), blocks[0], other, 0)
            else:
                for i in (1, 3, 2):
                    sender.send((chunk, 2, i), blocks[i], other, i)
            state[chunk] = blocks[0]
        else:
            if together:
                parts, others = *sender.take((chunk, 2, 0)), []
            else:
                parts, others = state[chunk], sender.take((chunk, 2, 1), (chunk, 2, 3), (chunk, 2, 2))
            hidden, squares, token = final(first, where, residual, parts, others, token)
            state[chunk] = (first, hidden, squares)
        sender.passed(step + chunk, token)
    done = sorted(state.values(), key=lambda entry: entry[0])
    hidden = jnp.concatenate([h for _, h, _ in done], axis=0)
    squares = jnp.concatenate([s for _, _, s in done], axis=0)[:, 0]
    widened = hidden.astype(jnp.float32)
    spread = jnp.tile(squares.reshape(8, -1), (X * Z, 1))
    spread = lax.all_to_all(spread, "tensor", split_axis=0, concat_axis=0, tiled=True)
    squares = jnp.sum(spread.reshape(X * Z, -1), axis=0)
    gain_part = lax.dynamic_slice_in_dim(norm_gain, tensor_index * feature_count, feature_count, 0)
    normed = (
        widened * lax.rsqrt(squares / D + EPSILON)[:, None] * gain_part.astype(jnp.float32)
    ).astype(jnp.bfloat16)
    return (hidden, normed)


def solution(mesh):
    placed = (P("dp", "tensor"), P(None, "dp", None), P("dp", "tensor"), P("tensor", None), P(), P())
    return jax.shard_map(
        body, mesh=mesh, in_specs=placed, out_specs=(P("dp", "tensor"), P("dp", "tensor")), check_vma=False
    )
```

```python
import functools
import math

import jax
import jax.numpy as jnp
from jax import lax
from jax.experimental import pallas as pl
from jax.experimental.pallas import tpu as pltpu
from jax.sharding import PartitionSpec as P

D = 4096
HEADS = 64
KVH = 8
HD = 128
SUB = 256
X = 4
Z = 4
WIDE = 256
MASK_FILL = -1e30
EPSILON = 1e-06
PLAN = {"B": (0, 384, "x", 1, True), "A": (384, 256, "z", 0, False), "C": (640, 384, "x", -1, False)}
ORDER = ("1B", "1A", "1C", "2B", "2A", "2C", "3B", "3A", "3C", "FB", "FA", "FC")
GATES = {("C", 1, "back"): "2C", ("A", 2, 1): "3C", ("A", 2, 2): "3C", ("A", 2, 3): "3C"}
COST = pl.CostEstimate(flops=1, bytes_accessed=1, transcendentals=0)
LONG = pl.CostEstimate(flops=200_000_000_000, bytes_accessed=1, transcendentals=0)
ATTEND_VMEM = 36 << 20
OTHER_VMEM = 16 << 20
TOKEN = jax.ShapeDtypeStruct((8, 128), jnp.float32)
ANY = pl.BlockSpec(memory_space=pl.ANY)
OWN, NEAR, FAR, BACK = 0, 1, 2, 3


def ring_pairs(axis, step):
    pairs = []
    for z in range(Z):
        for x in range(X):
            to = z * X + (x + step) % X if axis == "x" else (z + step) % Z * X + x
            pairs.append((z * X + x, to))
    return pairs


def shift(value, axis, step):
    return lax.ppermute(value, "tensor", ring_pairs(axis, step))


def swap(value, axis):
    if axis == "x":
        groups = [[z * X + x for x in range(X)] for z in range(Z)]
    else:
        groups = [[z * X + x for z in range(Z)] for x in range(X)]
    return lax.all_to_all(value, "tensor", split_axis=0, concat_axis=0, axis_index_groups=groups, tiled=True)


def full(shape):
    return pl.BlockSpec(shape, lambda i, s: (0,) * len(shape))


def call(kernel, name, cost, vmem, where, inputs, in_specs, out_shapes, scratch=()):
    return pl.pallas_call(
        kernel,
        out_shape=out_shapes,
        grid_spec=pltpu.PrefetchScalarGridSpec(
            num_scalar_prefetch=1,
            grid=(1,),
            in_specs=in_specs,
            out_specs=[full(o.shape) for o in out_shapes],
            scratch_shapes=list(scratch),
        ),
        compiler_params=pltpu.CompilerParams(vmem_limit_bytes=vmem),
        cost_estimate=cost,
        name=name,
    )(where, *inputs)


def columns_of(where_ref, axis, way, block):
    if way == 0:
        half = X * WIDE // 2
        wanted = {FAR: ((2, 0), (1, 1)), BACK: ((2, 1), (3, 0)), NEAR: ((1, 0), (3, 1)), OWN: ((0, 0), (0, 1))}[block]
        return [
            (pl.multiple_of(lax.rem(where_ref[2] + step, Z) * (X * WIDE) + side * half, half), half, i * half)
            for i, (step, side) in enumerate(wanted)
        ]
    size = X if axis == "x" else Z
    steps = block if way > 0 else (size - block) % size
    place = lax.rem(where_ref[3 if axis == "x" else 2] + steps, size)
    if axis == "x":
        return [(pl.multiple_of((z * X + place) * WIDE, WIDE), WIDE, z * WIDE) for z in range(Z)]
    return [(pl.multiple_of(place * (X * WIDE), X * WIDE), X * WIDE, 0)]


def attend_rows(first, rows, docs, q_ref, q_first, kv_ref):
    factor = math.log2(math.e) / math.sqrt(HD)
    q_docs = jnp.broadcast_to(docs[:, first : first + rows], (128, rows)).T[:, :1]
    tiles = [(start, min(SUB, first + rows - start)) for start in range(0, first + rows, SUB)]
    masks = []
    for start, width in tiles:
        mask = q_docs == docs[:, start : start + width]
        if start + width > first:
            here = (rows, width)
            ahead = lax.broadcasted_iota(jnp.int32, here, 1) - lax.broadcasted_iota(jnp.int32, here, 0)
            mask = mask & (ahead <= first - start)
        masks.append(mask)
    heads = []
    for head in range(q_ref.shape[1] // HD):
        q = q_ref[q_first : q_first + rows, head * HD : (head + 1) * HD]
        scores = []
        peak = None
        for (start, width), mask in zip(tiles, masks):
            keys = kv_ref[0, start : start + width, :]
            score = lax.dot_general(q, keys, (((1,), (1,)), ((), ())), preferred_element_type=jnp.float32)
            score = jnp.where(mask, score, MASK_FILL)
            top = jnp.max(score, axis=1, keepdims=True)
            peak = top if peak is None else jnp.maximum(peak, top)
            scores.append(score)
        offset = peak * factor
        total = 0.0
        summed = 0.0
        for (start, width), score in zip(tiles, scores):
            weight = jnp.exp2(score * factor - offset)
            total = total + jnp.sum(weight, axis=1, keepdims=True)
            summed = summed + jnp.dot(
                weight.astype(jnp.bfloat16), kv_ref[1, start : start + width, :], preferred_element_type=jnp.float32
            )
        heads.append((summed / total).astype(jnp.bfloat16))
    return jnp.concatenate(heads, axis=1)


def attend_kernel(first, rows, axis, way, inside, where_ref, token_ref, docs_hbm, q_hbm, kv_hbm, w_any, *rest):
    attn_ref, far_ref, back_ref, token_out, docs_ref, q_ref, kv_ref, sems, *more = rest
    keys = kv_ref.shape[1]
    column = pl.ds(pl.multiple_of(where_ref[0] * HD, HD), HD)
    fetches = [
        pltpu.make_async_copy(docs_hbm, docs_ref, sems.at[0]),
        pltpu.make_async_copy(q_hbm.at[pl.ds(first, rows), :], q_ref, sems.at[1]),
        pltpu.make_async_copy(kv_hbm.at[:, pl.ds(0, keys), column], kv_ref, sems.at[2]),
    ]
    for fetch in fetches:
        fetch.start()
    pieces = [columns_of(where_ref, axis, way, block) for block in (FAR, BACK)]
    later = [[], []]
    if not inside:
        w_ref, w_sems = more
        for slot in range(2):
            for i, (start, size, offset) in enumerate(pieces[slot]):
                later[slot].append(
                    pltpu.make_async_copy(
                        w_any.at[:, pl.ds(start, size)], w_ref.at[slot, :, offset : offset + size], w_sems.at[slot, i]
                    )
                )
                later[slot][-1].start()
    token_out[...] = jnp.zeros_like(token_out)
    for fetch in fetches:
        fetch.wait()
    docs = docs_ref[pl.ds(where_ref[1], 1), :]
    for at in range(0, rows, SUB):
        size = min(SUB, rows - at)
        attn_ref[at : at + size, :] = attend_rows(first + at, size, docs, q_ref, at, kv_ref)
    attn = attn_ref[...]
    for slot, out_ref in enumerate((far_ref, back_ref)):
        for fetch in later[slot]:
            fetch.wait()
        for start, size, offset in pieces[slot]:
            weight = w_any[:, pl.ds(start, size)] if inside else w_ref[slot, :, offset : offset + size]
            out_ref[:, offset : offset + size] = jnp.dot(attn, weight, preferred_element_type=jnp.float32).astype(
                jnp.bfloat16
            )


def attend(first, rows, axis, way, inside, where, docs, query, key_value, out_weight, token):
    cols = query.shape[1]
    keys = first + rows
    wide = out_weight.shape[1] // 4
    docs, query, key_value = [pltpu.with_memory_space_constraint(a, pltpu.HBM) for a in (docs, query, key_value)]
    out_weight = pltpu.with_memory_space_constraint(out_weight, pltpu.VMEM if inside else pltpu.HBM)
    scratch = [
        pltpu.VMEM(docs.shape, jnp.int32),
        pltpu.VMEM((rows, cols), jnp.bfloat16),
        pltpu.VMEM((2, keys, HD), jnp.bfloat16),
        pltpu.SemaphoreType.DMA((3,)),
    ]
    if not inside:
        scratch += [pltpu.VMEM((2, cols, wide), jnp.bfloat16), pltpu.SemaphoreType.DMA((2, 4))]
    return call(
        functools.partial(attend_kernel, first, rows, axis, way, inside),
        "attend_%d" % first,
        COST,
        ATTEND_VMEM,
        where,
        (token, docs, query, key_value, out_weight),
        [ANY] * 4 + [pl.BlockSpec(memory_space=pltpu.VMEM) if inside else ANY],
        [jax.ShapeDtypeStruct((rows, cols), jnp.bfloat16)]
        + [jax.ShapeDtypeStruct((rows, wide), jnp.bfloat16)] * 2
        + [TOKEN],
        scratch,
    )


def near_kernel(axis, way, where_ref, token_ref, w_ref, attn_ref, passed_ref, out_ref, own_ref, token_out):
    token_out[...] = jnp.zeros_like(token_out)
    for block in (NEAR, OWN):
        for start, size, offset in columns_of(where_ref, axis, way, block):
            total = jnp.dot(attn_ref[...], w_ref[:, pl.ds(start, size)], preferred_element_type=jnp.float32)
            if block == NEAR:
                total = total + passed_ref[:, offset : offset + size].astype(jnp.float32)
                out_ref[:, offset : offset + size] = total.astype(jnp.bfloat16)
            else:
                own_ref[:, offset : offset + size] = total.astype(jnp.bfloat16)


def near(axis, way, cost, where, out_weight, attn, passed, token):
    return call(
        functools.partial(near_kernel, axis, way),
        "near",
        cost,
        OTHER_VMEM,
        where,
        (token, pltpu.with_memory_space_constraint(out_weight, pltpu.VMEM), attn, passed),
        [ANY, pl.BlockSpec(memory_space=pltpu.VMEM), full(attn.shape), full(passed.shape)],
        [jax.ShapeDtypeStruct(passed.shape, jnp.bfloat16)] * 2 + [TOKEN],
    )


def both_kernel(where_ref, token_ref, w_ref, attn_ref, up_ref, down_ref, next_up, next_down, own_ref, token_out):
    token_out[...] = jnp.zeros_like(token_out)
    half = up_ref.shape[1] // 2
    for block in (NEAR, OWN):
        for i, (start, size, offset) in enumerate(columns_of(where_ref, "z", 0, block)):
            total = jnp.dot(attn_ref[...], w_ref[:, pl.ds(start, size)], preferred_element_type=jnp.float32)
            if block == NEAR:
                ref = (up_ref, down_ref)[i]
                (next_up, next_down)[i][...] = (total + ref[:, :half].astype(jnp.float32)).astype(jnp.bfloat16)
            else:
                ref = (down_ref, up_ref)[i]
                own_ref[:, offset : offset + size] = total + ref[:, half:].astype(jnp.float32)


def near_both(cost, where, out_weight, attn, up, down, token):
    rows, cols = up.shape
    halves = [jax.ShapeDtypeStruct((rows, cols // 2), jnp.bfloat16)] * 2
    return call(
        both_kernel,
        "near_both",
        cost,
        OTHER_VMEM,
        where,
        (token, pltpu.with_memory_space_constraint(out_weight, pltpu.VMEM), attn, up, down),
        [ANY, pl.BlockSpec(memory_space=pltpu.VMEM), full(attn.shape), full(up.shape), full(down.shape)],
        halves + [jax.ShapeDtypeStruct((rows, cols), jnp.float32), TOKEN],
    )


def merge_both_kernel(where_ref, token_ref, own_ref, up_ref, down_ref, *rest):
    outs, total_ref = rest[:-1], rest[-1]
    outs[-1][...] = jnp.zeros_like(outs[-1])
    half = up_ref.shape[1]
    total_ref[:, :half] = own_ref[:, :half] + up_ref[...].astype(jnp.float32)
    total_ref[:, half:] = own_ref[:, half:] + down_ref[...].astype(jnp.float32)
    for step in range(4):
        place = lax.rem(where_ref[3] + step, 4)
        cols = pl.ds(pl.multiple_of(place * WIDE, WIDE), WIDE)
        outs[step][...] = total_ref[:, cols].astype(jnp.bfloat16)


def merge_both(cost, where, own, up, down, token):
    rows = own.shape[0]
    return call(
        merge_both_kernel,
        "merge_both",
        cost,
        OTHER_VMEM,
        where,
        (token, own, up, down),
        [ANY] + [full(a.shape) for a in (own, up, down)],
        [jax.ShapeDtypeStruct((rows, WIDE), jnp.bfloat16)] * 4 + [TOKEN],
        [pltpu.VMEM(own.shape, jnp.float32)],
    )


def merge_kernel(axis, together, where_ref, token_ref, own_ref, ahead_ref, behind_ref, *outs):
    outs[-1][...] = jnp.zeros_like(outs[-1])
    for step in range(4):
        place = step if together else lax.rem(where_ref[2 if axis == "x" else 3] + step, 4)
        cols = pl.ds(pl.multiple_of(place * WIDE, WIDE), WIDE)
        total = own_ref[:, cols].astype(jnp.float32)
        for ref in (ahead_ref, behind_ref):
            total = total + ref[:, cols].astype(jnp.float32)
        if together:
            outs[0][step] = total.astype(jnp.bfloat16)
        else:
            outs[step][...] = total.astype(jnp.bfloat16)


def merge(axis, together, cost, where, own, ahead, behind, token):
    rows = own.shape[0]
    if together:
        blocks = [jax.ShapeDtypeStruct((4, rows, WIDE), jnp.bfloat16)]
    else:
        blocks = [jax.ShapeDtypeStruct((rows, WIDE), jnp.bfloat16)] * 4
    return call(
        functools.partial(merge_kernel, axis, together),
        "merge",
        cost,
        OTHER_VMEM,
        where,
        (token, own, ahead, behind),
        [ANY] + [full(own.shape)] * 3,
        blocks + [TOKEN],
    )


def final_kernel(where_ref, token_ref, residual_ref, parts_ref, *rest):
    others, (hidden_ref, squares_ref, token_out) = rest[:-3], rest[-3:]
    token_out[...] = jnp.zeros_like(token_out)
    if others:
        mixed = parts_ref[...].astype(jnp.float32)
        for ref in others:
            mixed = mixed + ref[...].astype(jnp.float32)
    else:
        mixed = parts_ref[0].astype(jnp.float32)
        for i in range(1, 4):
            mixed = mixed + parts_ref[i].astype(jnp.float32)
    hidden = (residual_ref[...].astype(jnp.float32) + mixed).astype(jnp.bfloat16)
    hidden_ref[...] = hidden
    widened = hidden.astype(jnp.float32)
    squares_ref[...] = jnp.sum(widened * widened, axis=1, keepdims=True)


def final(first, where, residual, parts, others, token):
    rows, cols = parts.shape[-2:]
    return call(
        final_kernel,
        "final",
        COST,
        OTHER_VMEM,
        where,
        (token, residual, parts, *others),
        [ANY, pl.BlockSpec((pl.Element(rows), pl.Element(cols)), lambda i, s: (first, 0))]
        + [full(a.shape) for a in (parts, *others)],
        [jax.ShapeDtypeStruct((rows, cols), jnp.bfloat16), jax.ShapeDtypeStruct((rows, 1), jnp.float32), TOKEN],
    )


class Sender:
    def __init__(self):
        self.tokens = {}
        self.held = {}
        self.results = {}

    def send(self, name, value, axis, way):
        gate = GATES.get(name)
        if gate is None or gate in self.tokens:
            if gate is not None:
                value, _ = lax.optimization_barrier((value, self.tokens[gate]))
            self.results[name] = shift(value, axis, way) if way else swap(value, axis)
        else:
            self.held[name] = (value, axis, way)

    def passed(self, step, token):
        self.tokens[step] = token
        for name in list(self.held):
            if GATES[name] == step:
                self.send(name, *self.held.pop(name))

    def take(self, *names):
        return [self.results[name] for name in names]


def body(query, key_value, residual, out_weight, norm_gain, doc_ids):
    tensor_index = lax.axis_index("tensor")
    group_index = lax.axis_index("dp")
    heads_here = query.shape[1] // HD
    kv_head = tensor_index * heads_here // (HEADS // KVH)
    where = jnp.stack([kv_head, group_index, tensor_index // X, tensor_index % X]).astype(jnp.int32)
    feature_count = residual.shape[1]
    token = where
    state = {}
    sender = Sender()
    for step, chunk in ORDER:
        first, rows, axis, way, together = PLAN[chunk]
        other = "z" if axis == "x" else "x"
        cost = LONG if chunk == "A" else COST
        if step == "1":
            inside = token is not where
            attn, far, back, token = attend(
                first, rows, axis, way, inside, where, doc_ids, query, key_value, out_weight, token
            )
            sender.send((chunk, 1, "far"), far, axis, way or 1)
            sender.send((chunk, 1, "back"), back, axis, -way or -1)
            state[chunk] = attn
        elif step == "2":
            attn = state[chunk]
            if chunk == "B":
                attn, _ = lax.optimization_barrier((attn, *sender.take((chunk, 1, "back"))))
            if way == 0:
                passed = sender.take((chunk, 1, "far"), (chunk, 1, "back"))
                up, down, state[chunk], token = near_both(cost, where, out_weight, attn, *passed, token)
                sender.send((chunk, 1, "up"), up, axis, 1)
                sender.send((chunk, 1, "down"), down, axis, -1)
                sender.passed(step + chunk, token)
                continue
            passed = sender.take((chunk, 1, "far"))
            summed, state[chunk], token = near(axis, way, cost, where, out_weight, attn, *passed, token)
            sender.send((chunk, 1, "near"), summed, axis, way)
        elif step == "3":
            if way == 0:
                others = sender.take((chunk, 1, "up"), (chunk, 1, "down"))
                *blocks, token = merge_both(cost, where, state[chunk], *others, token)
            else:
                others = sender.take((chunk, 1, "near"), (chunk, 1, "back"))
                *blocks, token = merge(axis, together, cost, where, state[chunk], *others, token)
            if together:
                sender.send((chunk, 2, 0), blocks[0], other, 0)
            else:
                for i in (1, 3, 2):
                    sender.send((chunk, 2, i), blocks[i], other, i)
            state[chunk] = blocks[0]
        else:
            if together:
                parts, others = *sender.take((chunk, 2, 0)), []
            else:
                parts, others = state[chunk], sender.take((chunk, 2, 1), (chunk, 2, 3), (chunk, 2, 2))
            hidden, squares, token = final(first, where, residual, parts, others, token)
            state[chunk] = (first, hidden, squares)
        sender.passed(step + chunk, token)
    done = sorted(state.values(), key=lambda entry: entry[0])
    hidden = jnp.concatenate([h for _, h, _ in done], axis=0)
    squares = jnp.concatenate([s for _, _, s in done], axis=0)[:, 0]
    widened = hidden.astype(jnp.float32)
    spread = jnp.tile(squares.reshape(8, -1), (X * Z, 1))
    spread = lax.all_to_all(spread, "tensor", split_axis=0, concat_axis=0, tiled=True)
    squares = jnp.sum(spread.reshape(X * Z, -1), axis=0)
    gain_part = lax.dynamic_slice_in_dim(norm_gain, tensor_index * feature_count, feature_count, 0)
    normed = (
        widened * lax.rsqrt(squares / D + EPSILON)[:, None] * gain_part.astype(jnp.float32)
    ).astype(jnp.bfloat16)
    return (hidden, normed)


def solution(mesh):
    placed = (P("dp", "tensor"), P(None, "dp", None), P("dp", "tensor"), P("tensor", None), P(), P())
    return jax.shard_map(
        body, mesh=mesh, in_specs=placed, out_specs=(P("dp", "tensor"), P("dp", "tensor")), check_vma=False
    )
```

```python
import functools
import math

import jax
import jax.numpy as jnp
from jax import lax
from jax.experimental import pallas as pl
from jax.experimental.pallas import tpu as pltpu
from jax.sharding import PartitionSpec as P

D = 4096
HEADS = 64
KVH = 8
HD = 128
SUB = 256
X = 4
Z = 4
WIDE = 256
MASK_FILL = -1e30
EPSILON = 1e-06
PLAN = {"B": (0, 384, "x", 1, False), "A": (384, 256, "z", 0, False), "C": (640, 384, "x", -1, False)}
ORDER = ("1B", "1A", "1C", "2B", "2A", "2C", "3B", "3A", "3C", "FB", "FA", "FC")
GATES = {("C", 1, "back"): "2C", ("A", 2, 1): "3C", ("A", 2, 2): "3C", ("A", 2, 3): "3C"}
COST = pl.CostEstimate(flops=1, bytes_accessed=1, transcendentals=0)
LONG = pl.CostEstimate(flops=200_000_000_000, bytes_accessed=1, transcendentals=0)
ATTEND_VMEM = 36 << 20
OTHER_VMEM = 16 << 20
TOKEN = jax.ShapeDtypeStruct((8, 128), jnp.float32)
ANY = pl.BlockSpec(memory_space=pl.ANY)
OWN, NEAR, FAR, BACK = 0, 1, 2, 3


def ring_pairs(axis, step):
    pairs = []
    for z in range(Z):
        for x in range(X):
            to = z * X + (x + step) % X if axis == "x" else (z + step) % Z * X + x
            pairs.append((z * X + x, to))
    return pairs


def shift(value, axis, step):
    return lax.ppermute(value, "tensor", ring_pairs(axis, step))


def swap(value, axis):
    if axis == "x":
        groups = [[z * X + x for x in range(X)] for z in range(Z)]
    else:
        groups = [[z * X + x for z in range(Z)] for x in range(X)]
    return lax.all_to_all(value, "tensor", split_axis=0, concat_axis=0, axis_index_groups=groups, tiled=True)


def full(shape):
    return pl.BlockSpec(shape, lambda i, s: (0,) * len(shape))


def call(kernel, name, cost, vmem, where, inputs, in_specs, out_shapes, scratch=()):
    return pl.pallas_call(
        kernel,
        out_shape=out_shapes,
        grid_spec=pltpu.PrefetchScalarGridSpec(
            num_scalar_prefetch=1,
            grid=(1,),
            in_specs=in_specs,
            out_specs=[full(o.shape) for o in out_shapes],
            scratch_shapes=list(scratch),
        ),
        compiler_params=pltpu.CompilerParams(vmem_limit_bytes=vmem),
        cost_estimate=cost,
        name=name,
    )(where, *inputs)


def columns_of(where_ref, axis, way, block):
    if way == 0:
        half = X * WIDE // 2
        wanted = {FAR: ((2, 0), (1, 1)), BACK: ((2, 1), (3, 0)), NEAR: ((1, 0), (3, 1)), OWN: ((0, 0), (0, 1))}[block]
        return [
            (pl.multiple_of(lax.rem(where_ref[2] + step, Z) * (X * WIDE) + side * half, half), half, i * half)
            for i, (step, side) in enumerate(wanted)
        ]
    size = X if axis == "x" else Z
    steps = block if way > 0 else (size - block) % size
    place = lax.rem(where_ref[3 if axis == "x" else 2] + steps, size)
    if axis == "x":
        return [(pl.multiple_of((z * X + place) * WIDE, WIDE), WIDE, z * WIDE) for z in range(Z)]
    return [(pl.multiple_of(place * (X * WIDE), X * WIDE), X * WIDE, 0)]


def attend_rows(first, rows, docs, q_ref, q_first, kv_ref):
    factor = math.log2(math.e) / math.sqrt(HD)
    q_docs = jnp.broadcast_to(docs[:, first : first + rows], (128, rows)).T[:, :1]
    tiles = [(start, min(SUB, first + rows - start)) for start in range(0, first + rows, SUB)]
    masks = []
    for start, width in tiles:
        mask = q_docs == docs[:, start : start + width]
        if start + width > first:
            here = (rows, width)
            ahead = lax.broadcasted_iota(jnp.int32, here, 1) - lax.broadcasted_iota(jnp.int32, here, 0)
            mask = mask & (ahead <= first - start)
        masks.append(mask)
    heads = []
    for head in range(q_ref.shape[1] // HD):
        q = q_ref[q_first : q_first + rows, head * HD : (head + 1) * HD]
        scores = []
        peak = None
        for (start, width), mask in zip(tiles, masks):
            keys = kv_ref[0, start : start + width, :]
            score = lax.dot_general(q, keys, (((1,), (1,)), ((), ())), preferred_element_type=jnp.float32)
            score = jnp.where(mask, score, MASK_FILL)
            top = jnp.max(score, axis=1, keepdims=True)
            peak = top if peak is None else jnp.maximum(peak, top)
            scores.append(score)
        offset = peak * factor
        total = 0.0
        summed = 0.0
        for (start, width), score in zip(tiles, scores):
            weight = jnp.exp2(score * factor - offset)
            total = total + jnp.sum(weight, axis=1, keepdims=True)
            summed = summed + jnp.dot(
                weight.astype(jnp.bfloat16), kv_ref[1, start : start + width, :], preferred_element_type=jnp.float32
            )
        heads.append((summed / total).astype(jnp.bfloat16))
    return jnp.concatenate(heads, axis=1)


def attend_kernel(first, rows, axis, way, inside, where_ref, token_ref, docs_hbm, q_hbm, kv_hbm, w_any, *rest):
    attn_ref, far_ref, back_ref, token_out, docs_ref, q_ref, kv_ref, sems, *more = rest
    keys = kv_ref.shape[1]
    column = pl.ds(pl.multiple_of(where_ref[0] * HD, HD), HD)
    fetches = [
        pltpu.make_async_copy(docs_hbm, docs_ref, sems.at[0]),
        pltpu.make_async_copy(q_hbm.at[pl.ds(first, rows), :], q_ref, sems.at[1]),
        pltpu.make_async_copy(kv_hbm.at[:, pl.ds(0, keys), column], kv_ref, sems.at[2]),
    ]
    for fetch in fetches:
        fetch.start()
    pieces = [columns_of(where_ref, axis, way, block) for block in (FAR, BACK)]
    later = [[], []]
    if not inside:
        w_ref, w_sems = more
        for slot in range(2):
            for i, (start, size, offset) in enumerate(pieces[slot]):
                later[slot].append(
                    pltpu.make_async_copy(
                        w_any.at[:, pl.ds(start, size)], w_ref.at[slot, :, offset : offset + size], w_sems.at[slot, i]
                    )
                )
                later[slot][-1].start()
    token_out[...] = jnp.zeros_like(token_out)
    for fetch in fetches:
        fetch.wait()
    docs = docs_ref[pl.ds(where_ref[1], 1), :]
    for at in range(0, rows, SUB):
        size = min(SUB, rows - at)
        attn_ref[at : at + size, :] = attend_rows(first + at, size, docs, q_ref, at, kv_ref)
    attn = attn_ref[...]
    for slot, out_ref in enumerate((far_ref, back_ref)):
        for fetch in later[slot]:
            fetch.wait()
        for start, size, offset in pieces[slot]:
            weight = w_any[:, pl.ds(start, size)] if inside else w_ref[slot, :, offset : offset + size]
            out_ref[:, offset : offset + size] = jnp.dot(attn, weight, preferred_element_type=jnp.float32).astype(
                jnp.bfloat16
            )


def attend(first, rows, axis, way, inside, where, docs, query, key_value, out_weight, token):
    cols = query.shape[1]
    keys = first + rows
    wide = out_weight.shape[1] // 4
    docs, query, key_value = [pltpu.with_memory_space_constraint(a, pltpu.HBM) for a in (docs, query, key_value)]
    out_weight = pltpu.with_memory_space_constraint(out_weight, pltpu.VMEM if inside else pltpu.HBM)
    scratch = [
        pltpu.VMEM(docs.shape, jnp.int32),
        pltpu.VMEM((rows, cols), jnp.bfloat16),
        pltpu.VMEM((2, keys, HD), jnp.bfloat16),
        pltpu.SemaphoreType.DMA((3,)),
    ]
    if not inside:
        scratch += [pltpu.VMEM((2, cols, wide), jnp.bfloat16), pltpu.SemaphoreType.DMA((2, 4))]
    return call(
        functools.partial(attend_kernel, first, rows, axis, way, inside),
        "attend_%d" % first,
        COST,
        ATTEND_VMEM,
        where,
        (token, docs, query, key_value, out_weight),
        [ANY] * 4 + [pl.BlockSpec(memory_space=pltpu.VMEM) if inside else ANY],
        [jax.ShapeDtypeStruct((rows, cols), jnp.bfloat16)]
        + [jax.ShapeDtypeStruct((rows, wide), jnp.bfloat16)] * 2
        + [TOKEN],
        scratch,
    )


def near_kernel(axis, way, where_ref, token_ref, w_ref, attn_ref, passed_ref, out_ref, own_ref, token_out):
    token_out[...] = jnp.zeros_like(token_out)
    for block in (NEAR, OWN):
        for start, size, offset in columns_of(where_ref, axis, way, block):
            total = jnp.dot(attn_ref[...], w_ref[:, pl.ds(start, size)], preferred_element_type=jnp.float32)
            if block == NEAR:
                total = total + passed_ref[:, offset : offset + size].astype(jnp.float32)
                out_ref[:, offset : offset + size] = total.astype(jnp.bfloat16)
            else:
                own_ref[:, offset : offset + size] = total.astype(jnp.bfloat16)


def near(axis, way, cost, where, out_weight, attn, passed, token):
    return call(
        functools.partial(near_kernel, axis, way),
        "near",
        cost,
        OTHER_VMEM,
        where,
        (token, pltpu.with_memory_space_constraint(out_weight, pltpu.VMEM), attn, passed),
        [ANY, pl.BlockSpec(memory_space=pltpu.VMEM), full(attn.shape), full(passed.shape)],
        [jax.ShapeDtypeStruct(passed.shape, jnp.bfloat16)] * 2 + [TOKEN],
    )


def both_kernel(where_ref, token_ref, w_ref, attn_ref, up_ref, down_ref, next_up, next_down, own_ref, token_out):
    token_out[...] = jnp.zeros_like(token_out)
    half = up_ref.shape[1] // 2
    for block in (NEAR, OWN):
        for i, (start, size, offset) in enumerate(columns_of(where_ref, "z", 0, block)):
            total = jnp.dot(attn_ref[...], w_ref[:, pl.ds(start, size)], preferred_element_type=jnp.float32)
            if block == NEAR:
                ref = (up_ref, down_ref)[i]
                (next_up, next_down)[i][...] = (total + ref[:, :half].astype(jnp.float32)).astype(jnp.bfloat16)
            else:
                ref = (down_ref, up_ref)[i]
                own_ref[:, offset : offset + size] = total + ref[:, half:].astype(jnp.float32)


def near_both(cost, where, out_weight, attn, up, down, token):
    rows, cols = up.shape
    halves = [jax.ShapeDtypeStruct((rows, cols // 2), jnp.bfloat16)] * 2
    return call(
        both_kernel,
        "near_both",
        cost,
        OTHER_VMEM,
        where,
        (token, pltpu.with_memory_space_constraint(out_weight, pltpu.VMEM), attn, up, down),
        [ANY, pl.BlockSpec(memory_space=pltpu.VMEM), full(attn.shape), full(up.shape), full(down.shape)],
        halves + [jax.ShapeDtypeStruct((rows, cols), jnp.float32), TOKEN],
    )


def merge_both_kernel(where_ref, token_ref, own_ref, up_ref, down_ref, *rest):
    outs, total_ref = rest[:-1], rest[-1]
    outs[-1][...] = jnp.zeros_like(outs[-1])
    half = up_ref.shape[1]
    total_ref[:, :half] = own_ref[:, :half] + up_ref[...].astype(jnp.float32)
    total_ref[:, half:] = own_ref[:, half:] + down_ref[...].astype(jnp.float32)
    for step in range(4):
        place = lax.rem(where_ref[3] + step, 4)
        cols = pl.ds(pl.multiple_of(place * WIDE, WIDE), WIDE)
        outs[step][...] = total_ref[:, cols].astype(jnp.bfloat16)


def merge_both(cost, where, own, up, down, token):
    rows = own.shape[0]
    return call(
        merge_both_kernel,
        "merge_both",
        cost,
        OTHER_VMEM,
        where,
        (token, own, up, down),
        [ANY] + [full(a.shape) for a in (own, up, down)],
        [jax.ShapeDtypeStruct((rows, WIDE), jnp.bfloat16)] * 4 + [TOKEN],
        [pltpu.VMEM(own.shape, jnp.float32)],
    )


def merge_kernel(axis, together, where_ref, token_ref, own_ref, ahead_ref, behind_ref, *outs):
    outs[-1][...] = jnp.zeros_like(outs[-1])
    for step in range(4):
        place = step if together else lax.rem(where_ref[2 if axis == "x" else 3] + step, 4)
        cols = pl.ds(pl.multiple_of(place * WIDE, WIDE), WIDE)
        total = own_ref[:, cols].astype(jnp.float32)
        for ref in (ahead_ref, behind_ref):
            total = total + ref[:, cols].astype(jnp.float32)
        if together:
            outs[0][step] = total.astype(jnp.bfloat16)
        else:
            outs[step][...] = total.astype(jnp.bfloat16)


def merge(axis, together, cost, where, own, ahead, behind, token):
    rows = own.shape[0]
    if together:
        blocks = [jax.ShapeDtypeStruct((4, rows, WIDE), jnp.bfloat16)]
    else:
        blocks = [jax.ShapeDtypeStruct((rows, WIDE), jnp.bfloat16)] * 4
    return call(
        functools.partial(merge_kernel, axis, together),
        "merge",
        cost,
        OTHER_VMEM,
        where,
        (token, own, ahead, behind),
        [ANY] + [full(own.shape)] * 3,
        blocks + [TOKEN],
    )


def final_kernel(where_ref, token_ref, residual_ref, parts_ref, *rest):
    others, (hidden_ref, squares_ref, token_out) = rest[:-3], rest[-3:]
    token_out[...] = jnp.zeros_like(token_out)
    if others:
        mixed = parts_ref[...].astype(jnp.float32)
        for ref in others:
            mixed = mixed + ref[...].astype(jnp.float32)
    else:
        mixed = parts_ref[0].astype(jnp.float32)
        for i in range(1, 4):
            mixed = mixed + parts_ref[i].astype(jnp.float32)
    hidden = (residual_ref[...].astype(jnp.float32) + mixed).astype(jnp.bfloat16)
    hidden_ref[...] = hidden
    widened = hidden.astype(jnp.float32)
    squares_ref[...] = jnp.sum(widened * widened, axis=1, keepdims=True)


def final(first, where, residual, parts, others, token):
    rows, cols = parts.shape[-2:]
    return call(
        final_kernel,
        "final",
        COST,
        OTHER_VMEM,
        where,
        (token, residual, parts, *others),
        [ANY, pl.BlockSpec((pl.Element(rows), pl.Element(cols)), lambda i, s: (first, 0))]
        + [full(a.shape) for a in (parts, *others)],
        [jax.ShapeDtypeStruct((rows, cols), jnp.bfloat16), jax.ShapeDtypeStruct((rows, 1), jnp.float32), TOKEN],
    )


class Sender:
    def __init__(self):
        self.tokens = {}
        self.held = {}
        self.results = {}

    def send(self, name, value, axis, way):
        gate = GATES.get(name)
        if gate is None or gate in self.tokens:
            if gate is not None:
                value, _ = lax.optimization_barrier((value, self.tokens[gate]))
            self.results[name] = shift(value, axis, way) if way else swap(value, axis)
        else:
            self.held[name] = (value, axis, way)

    def passed(self, step, token):
        self.tokens[step] = token
        for name in list(self.held):
            if GATES[name] == step:
                self.send(name, *self.held.pop(name))

    def take(self, *names):
        return [self.results[name] for name in names]


def body(query, key_value, residual, out_weight, norm_gain, doc_ids):
    tensor_index = lax.axis_index("tensor")
    group_index = lax.axis_index("dp")
    heads_here = query.shape[1] // HD
    kv_head = tensor_index * heads_here // (HEADS // KVH)
    where = jnp.stack([kv_head, group_index, tensor_index // X, tensor_index % X]).astype(jnp.int32)
    feature_count = residual.shape[1]
    token = where
    state = {}
    sender = Sender()
    for step, chunk in ORDER:
        first, rows, axis, way, together = PLAN[chunk]
        other = "z" if axis == "x" else "x"
        cost = LONG if chunk == "A" else COST
        if step == "1":
            inside = token is not where
            attn, far, back, token = attend(
                first, rows, axis, way, inside, where, doc_ids, query, key_value, out_weight, token
            )
            sender.send((chunk, 1, "far"), far, axis, way or 1)
            sender.send((chunk, 1, "back"), back, axis, -way or -1)
            state[chunk] = attn
        elif step == "2":
            attn = state[chunk]
            if chunk == "B":
                attn, _ = lax.optimization_barrier((attn, *sender.take((chunk, 1, "back"))))
            if way == 0:
                passed = sender.take((chunk, 1, "far"), (chunk, 1, "back"))
                up, down, state[chunk], token = near_both(cost, where, out_weight, attn, *passed, token)
                sender.send((chunk, 1, "up"), up, axis, 1)
                sender.send((chunk, 1, "down"), down, axis, -1)
                sender.passed(step + chunk, token)
                continue
            passed = sender.take((chunk, 1, "far"))
            summed, state[chunk], token = near(axis, way, cost, where, out_weight, attn, *passed, token)
            sender.send((chunk, 1, "near"), summed, axis, way)
        elif step == "3":
            if way == 0:
                others = sender.take((chunk, 1, "up"), (chunk, 1, "down"))
                *blocks, token = merge_both(cost, where, state[chunk], *others, token)
            else:
                others = sender.take((chunk, 1, "near"), (chunk, 1, "back"))
                *blocks, token = merge(axis, together, cost, where, state[chunk], *others, token)
            if together:
                sender.send((chunk, 2, 0), blocks[0], other, 0)
            else:
                for i in (1, 3, 2):
                    sender.send((chunk, 2, i), blocks[i], other, i)
            state[chunk] = blocks[0]
        else:
            if together:
                parts, others = *sender.take((chunk, 2, 0)), []
            else:
                parts, others = state[chunk], sender.take((chunk, 2, 1), (chunk, 2, 3), (chunk, 2, 2))
            hidden, squares, token = final(first, where, residual, parts, others, token)
            state[chunk] = (first, hidden, squares)
        sender.passed(step + chunk, token)
    done = sorted(state.values(), key=lambda entry: entry[0])
    hidden = jnp.concatenate([h for _, h, _ in done], axis=0)
    squares = jnp.concatenate([s for _, _, s in done], axis=0)[:, 0]
    widened = hidden.astype(jnp.float32)
    spread = jnp.tile(squares.reshape(8, -1), (X * Z, 1))
    spread = lax.all_to_all(spread, "tensor", split_axis=0, concat_axis=0, tiled=True)
    squares = jnp.sum(spread.reshape(X * Z, -1), axis=0)
    gain_part = lax.dynamic_slice_in_dim(norm_gain, tensor_index * feature_count, feature_count, 0)
    normed = (
        widened * lax.rsqrt(squares / D + EPSILON)[:, None] * gain_part.astype(jnp.float32)
    ).astype(jnp.bfloat16)
    return (hidden, normed)


def solution(mesh):
    placed = (P("dp", "tensor"), P(None, "dp", None), P("dp", "tensor"), P("tensor", None), P(), P())
    return jax.shard_map(
        body, mesh=mesh, in_specs=placed, out_specs=(P("dp", "tensor"), P("dp", "tensor")), check_vma=False
    )
```
